128 devices in a mesh: cluster: 4 (over y_lo, core), sub: 32 (over z, y_hi, x).
Axes of the slice: x: 4, y: 4 (y_hi: 2, y_lo: 2; y = y_hi * 2 + y_lo), z: 4, core: 2. Of those that a mesh axis runs over, the one named last changes fastest.
Arguments:
- load: float32 [229376, 256], P(('cluster', 'sub'))
- schur: float32 [229376, 1792], P(('cluster', 'sub')), as said below
- modes: float32 [229376, 128], P(('cluster', 'sub')), may hold values from -0.125 to 0.125
- coarse_inverse: float32 [16384, 4096], P(('cluster', 'sub')), as said below
- interface_rows: int32 [128], P(('cluster', 'sub')), may hold values from 896 to 1792, as said below
- mode_count: int32 [128], P(('cluster', 'sub')), may hold values from 64 to 128, as said below
- left_rows: int32 [128, 384], P(('cluster', 'sub')), may hold values from 0 to 1792, as said below
- right_rows: int32 [128, 384], P(('cluster', 'sub')), may hold values from 0 to 1792, as said below
Outputs:
- solution: float32 [229376, 256], P(('cluster', 'sub'))
- residual: float32 [229376, 256], P(('cluster', 'sub'))
The draws below stay inside these ranges and needn't reach their ends.
Inputs may be any that keep to these rules, and one draw needn't show every extreme that they name: `interface_rows`: every subdomain has at least half of 1792 live rows, and some subdomain has exactly 1792. `mode_count`: every subdomain has at least half of 128 live modes, and some subdomain has exactly 128. Slot j of right_rows[g] and slot j of left_rows[g + 1] name the same interface unknown; the used slots of a row come first, all other slots hold 1792. Two neighbours share at least half of 384 rows and some pair shares exactly 384. The used entries of left_rows[g] and right_rows[g] are distinct live rows of g. left_rows[0] and right_rows[127] are unused. `right_rows`: see left_rows. `schur`: each block S_g is symmetric positive definite with a positive diagonal. `coarse_inverse`: each cluster's coarse inverse is symmetric positive definite.
All inputs are finite; a program needn't handle non-finite values.
Results may differ from the reference program's by a relative error of at most 0.0001.
Values sent between devices are 32-bit elements; how exact they have to be, the bound alone decides.
A program may use at most 128 MiB of HBM per device.

```python
import math
import jax
import jax.numpy as jnp
from jax import lax

NI = 1792
NS = 384
K = 256
NM = 128
ITERS = 3
CLUSTERS = 4
SUBS = 128
CO = 4096


def interface_layout(key):
    base = jax.random.fold_in(key, 11)
    subkeys = jax.random.split(base, 5)
    orders = jax.random.randint(subkeys[0], (SUBS,), NI // 2, NI + 1)
    orders = orders.at[jax.random.randint(subkeys[1], (), 0, SUBS)].set(NI)
    shared = jax.random.randint(subkeys[2], (SUBS - 1,), NS // 2, NS + 1)
    shared = shared.at[jax.random.randint(subkeys[3], (), 0, SUBS - 1)].set(NS)
    nothing = jnp.zeros((1,), jnp.int32)
    right_count = jnp.concatenate([shared, nothing])
    left_count = jnp.concatenate([nothing, shared])
    scores = jax.random.randint(subkeys[4], (SUBS, NI), 0, 1048576)
    positions = jnp.arange(NI, dtype=jnp.int32)
    ranked = jnp.where(positions[None, :] < orders[:, None], scores, 1048576) * NI + positions[None, :]
    picked = jnp.argsort(ranked, axis=1, stable=True)[:, :2 * NS].astype(jnp.int32)
    slots = jnp.arange(NS, dtype=jnp.int32)
    right_index = jnp.where(slots[None, :] < right_count[:, None], picked[:, :NS], NI)
    left_index = jnp.where(slots[None, :] < left_count[:, None], picked[:, NS:], NI)
    return (orders.astype(jnp.int32), left_index.astype(jnp.int32), right_index.astype(jnp.int32))


def draw_interface_rows(key, part):
    return interface_layout(key)[0]


def draw_left_rows(key, part):
    return interface_layout(key)[1]


def draw_right_rows(key, part):
    return interface_layout(key)[2]


def draw_mode_count(key, part):
    base = jax.random.fold_in(key, 23)
    first_key, second_key = jax.random.split(base)
    counts = jax.random.randint(first_key, (SUBS,), NM // 2, NM + 1)
    counts = counts.at[jax.random.randint(second_key, (), 0, SUBS)].set(NM)
    return counts.astype(jnp.int32)


def draw_schur(key, part):
    base = jax.random.fold_in(key, 31)

    def single(index):
        sub_key = jax.random.fold_in(base, index)
        noise_key, diag_key = jax.random.split(sub_key)
        raw = jax.random.normal(noise_key, (NI, NI), jnp.float32) * (0.8 / math.sqrt(NI))
        diagonal = jax.random.uniform(diag_key, (NI,), jnp.float32, 3.0, 6.0)
        return raw + raw.T + jnp.diag(diagonal)
    return lax.map(single, jnp.arange(SUBS)).reshape(SUBS * NI, NI)


def draw_coarse_inverse(key, part):
    base = jax.random.fold_in(key, 37)

    def single(index):
        sub_key = jax.random.fold_in(base, index)
        noise_key, diag_key = jax.random.split(sub_key)
        raw = jax.random.normal(noise_key, (CO, CO), jnp.float32) * (0.25 / math.sqrt(CO))
        diagonal = jax.random.uniform(diag_key, (CO,), jnp.float32, 1.0, 2.0)
        return raw + raw.T + jnp.diag(diagonal)
    return lax.map(single, jnp.arange(CLUSTERS)).reshape(CLUSTERS * CO, CO)


def draw_load(key, part):
    base = jax.random.fold_in(key, 41)
    subkeys = jax.random.split(base, 1)
    ramp = 1.0 + 2.0 * jnp.arange(SUBS, dtype=jnp.float32) / max(SUBS - 1, 1)
    values = jax.random.normal(subkeys[0], (SUBS, NI, K), jnp.float32)
    return (values * ramp[:, None, None]).reshape(SUBS * NI, K)


def block_scale(stream_key, dims, pieces, low, top_value):
    def one(dim, shards_of):
        draws = jax.random.uniform(jax.random.fold_in(jax.random.fold_in(stream_key, 6), dim), (shards_of,), jnp.float32, low / len(pieces), top_value / len(pieces))
        return jnp.repeat(jnp.exp(draws), dims[dim] // shards_of).reshape((-1,) + (1,) * (len(dims) - dim - 1))

    level = one(*pieces[0])
    for cut in pieces[1:]:
        level = level * one(*cut)
    return level


def scatter_about(key, extent, width, most, cuts=(), held_as=jnp.bfloat16):
    entries = jax.random.normal(key, extent, jnp.float32) * width
    if len(cuts) > 0:
        entries = block_scale(key, extent, cuts, -0.22, 0.18) * entries
    return jnp.clip(entries, min=-most, max=most).astype(held_as)


def setup_inputs(seed: int = 0) -> dict:
    arg_keys = jax.random.split(jax.random.key(seed), 9)
    return {
        "load": draw_load(jax.random.fold_in(arg_keys[8], 71), 0),
        "schur": draw_schur(jax.random.fold_in(arg_keys[8], 71), 0),
        "modes": scatter_about(arg_keys[2], (SUBS * NI, NM), NI ** -0.5, 0.125, ((0, 128),), jnp.float32),
        "coarse_inverse": draw_coarse_inverse(jax.random.fold_in(arg_keys[8], 71), 0),
        "interface_rows": draw_interface_rows(jax.random.fold_in(arg_keys[8], 71), 0),
        "mode_count": draw_mode_count(jax.random.fold_in(arg_keys[8], 71), 0),
        "left_rows": draw_left_rows(jax.random.fold_in(arg_keys[8], 71), 0),
        "right_rows": draw_right_rows(jax.random.fold_in(arg_keys[8], 71), 0),
    }


def take_rows(field, indices):
    return jnp.take(field, indices, axis=0, mode="fill", fill_value=0.0)


def add_rows(field, indices, values):
    return field.at[indices].add(values, mode="drop")


def assemble(field, left_rows, right_rows):
    to_left = jax.vmap(take_rows)(field, left_rows)
    to_right = jax.vmap(take_rows)(field, right_rows)
    nothing = jnp.zeros_like(to_left[:1])
    from_left = jnp.concatenate([nothing, to_right[:-1]], 0)
    from_right = jnp.concatenate([to_left[1:], nothing], 0)
    merged = jax.vmap(add_rows)(field, left_rows, from_left)
    return jax.vmap(add_rows)(merged, right_rows, from_right)


def schur_apply(operands):
    return jnp.dot(operands[0], operands[1], precision=lax.Precision.HIGHEST, preferred_element_type=jnp.float32)


def reference(load, schur, modes, coarse_inverse, interface_rows, mode_count, left_rows, right_rows):
    highest = lax.Precision.HIGHEST
    load_blocks = load.reshape(SUBS, NI, K)
    schur_blocks = schur.reshape(SUBS, NI, NI)
    mode_blocks = modes.reshape(SUBS, NI, NM)
    coarse_blocks = coarse_inverse.reshape(CLUSTERS, CO, CO)
    positions = jnp.arange(NI, dtype=jnp.int32)
    live = (positions[None, :] < interface_rows[:, None]).astype(jnp.float32)
    ones_shared = jnp.ones((NS,), jnp.float32)

    def multiplicity(left_index, right_index):
        counted = jnp.zeros((NI,), jnp.float32).at[left_index].add(ones_shared, mode="drop")
        return counted.at[right_index].add(ones_shared, mode="drop")

    counts = jax.vmap(multiplicity)(left_rows, right_rows)
    share = live / (1.0 + counts)
    mode_live = (jnp.arange(NM, dtype=jnp.int32)[None, :] < mode_count[:, None]).astype(jnp.float32)
    schur_diag = jnp.diagonal(schur_blocks, axis1=1, axis2=2)
    rhs = assemble(live[:, :, None] * load_blocks, left_rows, right_rows)
    solution = jnp.zeros_like(rhs)
    residual = rhs
    for iteration in range(ITERS):
        modal = jnp.einsum("gim,gik->gmk", mode_blocks, share[:, :, None] * residual, precision=highest)
        modal = modal * mode_live[:, :, None]
        stacked = modal.reshape(CLUSTERS, CO, K)
        correction = jnp.einsum("cij,cjk->cik", coarse_blocks, stacked, precision=highest)
        correction = correction.reshape(SUBS, NM, K) * mode_live[:, :, None]
        prolonged = jnp.einsum("gim,gmk->gik", mode_blocks, correction, precision=highest)
        local_part = share[:, :, None] * (prolonged + residual / schur_diag[:, :, None])
        direction = assemble(local_part, left_rows, right_rows)
        product = lax.map(schur_apply, (schur_blocks, direction))
        image = assemble(live[:, :, None] * product, left_rows, right_rows)
        numerator = jnp.sum(share[:, :, None] * residual * image, axis=(0, 1))
        denominator = jnp.sum(share[:, :, None] * image * image, axis=(0, 1))
        alpha = numerator / (denominator + 1e-6)
        solution = solution + alpha[None, None, :] * direction
        residual = residual - alpha[None, None, :] * image
    return solution.reshape(SUBS * NI, K), residual.reshape(SUBS * NI, K)
```

```python
import functools

import jax
import jax.numpy as jnp
from jax import lax
from jax.experimental import pallas as pl
from jax.experimental.pallas import tpu as pltpu
from jax.sharding import PartitionSpec as P

MESH = pl.DeviceIdType.MESH
F32 = jnp.float32
BF16 = jnp.bfloat16
NI = 1792
NS = 384
K = 256
NM = 128
ITERS = 3
W = 128
STREAMS = K // W
TILE = 256
ROW_TILES = NI // TILE
CHUNK = 128
CHUNKS = NI // CHUNK

ZY = [(2, 1), (2, 0), (1, 1), (3, 1), (1, 0), (3, 0), (0, 1), (0, 0)]
YC = [(dy, dc) for dy in (2, 1, 3, 0) for dc in (1, 0) if (dy, dc) != (0, 0)]
THREE = (2, 1, 3)


def split(value):
    high = value.astype(BF16)
    low = (value - high.astype(F32)).astype(BF16)
    return jnp.concatenate([high, low], axis=1)


def halves(value):
    width = value.shape[1] // 2
    return value[:, :width] + value[:, width:]


def dot(a, b):
    return jnp.dot(a, b, preferred_element_type=F32)


def each_tile(count, size, body):
    def step(i, carry):
        body(pl.ds(pl.multiple_of(i * size, size), size), i * size)
        return carry

    lax.fori_loop(0, count, step, 0)


def kernel(
    load, schur, modes, coarse, live_rows, mode_count, index_row, index_column,
    x_out, r_out,
    s_hi, s_lo, ss_hi, ss_lo, chunk, to_slots, from_slots, phi, phit_hi, phit_lo, phi3_hi, phi3_lo,
    c_in, c_hi, c_lo, share, delta, pair_send, pair_recv,
    w_buf, d_buf, two, e_send, e_recv, ag, ag_two, rs_send, rs_recv, corr, corr_w, corr_two, ar_send, ar_recv,
    local_sem, chunk_sem, send_sem, recv_sem,
):
    c = lax.axis_index("cluster")
    s = lax.axis_index("sub")
    z, yh, xx = s // 8, (s // 4) % 2, s % 4
    g = c * 32 + s

    def ring(by):
        t = (g + by + 128) % 128
        return (t // 32, t % 32)

    def x_peer(dx):
        return (c, z * 8 + yh * 4 + (xx + dx) % 4)

    def zy_line(dz, dy):
        return ((z + dz) % 4) * 2 + (yh + dy) % 2

    def zy_peer(dz, dy):
        return (c, zy_line(dz, dy) * 4 + xx)

    def yc_peer(dy, dc):
        y = (yh * 2 + c // 2 + dy) % 4
        return ((y % 2) * 2 + (c + dc) % 2, z * 8 + (y // 2) * 4 + xx)

    def back(dz, dy):
        return ZY.index(((4 - dz) % 4, (2 - dy) % 2))

    counter = [0]
    started = []

    def send(src, dst, peer):
        n = counter[0]
        counter[0] = n + 1
        copy = pltpu.make_async_remote_copy(
            src_ref=src, dst_ref=dst, send_sem=send_sem.at[n], recv_sem=recv_sem.at[n],
            device_id=peer, device_id_type=MESH,
        )
        copy.start()
        return copy

    loads = [
        pltpu.make_async_copy(load.at[:, pl.ds(h * W, W)], w_buf.at[h], local_sem.at[h])
        for h in range(STREAMS)
    ]
    loads.append(pltpu.make_async_copy(modes, phi, local_sem.at[STREAMS]))
    line = z * 2 + yh
    loads.append(
        pltpu.make_async_copy(
            coarse.at[:, pl.ds(pl.multiple_of(line * 512, 512), 512)], c_in.at[7], local_sem.at[STREAMS + 1]
        )
    )
    for copy in loads:
        copy.start()

    def chunk_copy(i):
        slot = lax.rem(i, 2)
        return pltpu.make_async_copy(
            schur.at[pl.ds(pl.multiple_of(i * CHUNK, CHUNK), CHUNK)], chunk.at[slot], chunk_sem.at[slot]
        )

    chunk_copy(0).start()
    chunk_copy(1).start()

    peers = [ring(1), ring(-1)]
    peers += [x_peer(d) for d in THREE]
    peers += [zy_peer(*d) for d in ZY[:-1]]
    peers += [yc_peer(*d) for d in YC]
    barrier = pltpu.get_barrier_semaphore()
    for peer in peers:
        pl.semaphore_signal(barrier, inc=1, device_id=peer, device_id_type=MESH)

    live_count = live_rows[0]
    modes_live = mode_count[0]

    def build_slots(rows, base):
        local = lax.broadcasted_iota(jnp.int32, (TILE, NI), 1)
        from_slots[rows] = (local == index_column[rows]).astype(F32).astype(BF16)

    each_tile(2 * NS // TILE, TILE, build_slots)

    def live_mask(base, shape):
        return (lax.broadcasted_iota(jnp.int32, shape, 0) + base) < live_count

    for h in range(STREAMS):
        loads[h].wait()

        def mask_load(rows, base, h=h):
            value = jnp.where(live_mask(base, (TILE, W)), w_buf[h, rows], 0.0)
            w_buf[h, rows] = value
            two[h, rows] = split(value)

        each_tile(ROW_TILES, TILE, mask_load)

    pl.semaphore_wait(barrier, len(peers))

    c_copies = [
        send(
            coarse.at[:, pl.ds(pl.multiple_of(zy_line(dz, dy) * 512, 512), 512)],
            c_in.at[back(dz, dy)],
            zy_peer(dz, dy),
        )
        for dz, dy in ZY[:-1]
    ]

    def exchange(src, dst):
        return [
            send(src.at[pl.ds(NS, NS)], dst.at[pl.ds(0, NS)], ring(1)),
            send(src.at[pl.ds(0, NS)], dst.at[pl.ds(NS, NS)], ring(-1)),
        ]

    def arrived(copies):
        for copy in copies:
            copy.wait_recv()

    def left(copies):
        for copy in copies:
            copy.wait_send()

    def zeros8():
        return jnp.zeros((8, W), F32)

    def fold8(value):
        return jnp.sum(value.reshape(TILE // 8, 8, W), axis=0)

    def stream(h):
        e_copies = []

        def send_shared(t):
            e_copies.append(exchange(e_send.at[h], e_recv.at[h, t]))

        def gather_load(rows, base):
            e_send[h, rows] = halves(dot(from_slots[rows], two[h]))

        each_tile(2 * NS // TILE, TILE, gather_load)
        send_shared(0)
        yield

        def receive_shared(t):
            arrived(e_copies[t])

            def cut(rows, base):
                e_two_rows = split(e_recv[h, t, rows])
                e_two[rows] = e_two_rows

            each_tile(2 * NS // TILE, TILE, cut)

        e_two = two.at[STREAMS]

        def scattered(rows):
            return halves(dot(to_slots[rows], e_two[pl.ds(0, 2 * NS)]))

        def modal_and_gather(t):
            modal = halves(dot(phit_hi[...], two[h]) + dot(phit_lo[...], two[h]))
            ag[h, t, xx] = modal
            return [send(ag.at[h, t, xx], ag.at[h, t, xx], x_peer(d)) for d in THREE]

        receive_shared(0)

        def first_residual(rows, base):
            value = w_buf[h, rows] + scattered(rows)
            r_out[rows, pl.ds(h * W, W)] = value
            two[h, rows] = split(value)

        each_tile(ROW_TILES, TILE, first_residual)
        ag_copies = modal_and_gather(0)
        yield

        def reduce_x(t):
            return [send(ar_send.at[h, t, 0], ar_recv.at[h, t, i], x_peer(d)) for i, d in enumerate(THREE)]

        def reduce_z(t, copies):
            arrived(copies)
            ar_send[h, t, 1] = ar_send[h, t, 0] + ar_recv[h, t, 0] + ar_recv[h, t, 1] + ar_recv[h, t, 2]
            return [send(ar_send.at[h, t, 1], ar_recv.at[h, t, 3 + i], zy_peer(d, 0)) for i, d in enumerate(THREE)]

        def reduce_y(t, copies):
            arrived(copies)
            ar_send[h, t, 2] = ar_send[h, t, 1] + ar_recv[h, t, 3] + ar_recv[h, t, 4] + ar_recv[h, t, 5]
            return [send(ar_send.at[h, t, 2], ar_recv.at[h, t, 6 + i], yc_peer(*d)) for i, d in enumerate(YC)]

        def reduced(t, copies):
            arrived(copies)
            total = ar_send[h, t, 2]
            for i in range(7):
                total = total + ar_recv[h, t, 6 + i]
            numerator = jnp.sum(total[:8], axis=0, keepdims=True)
            denominator = jnp.sum(total[8:], axis=0, keepdims=True)
            return numerator / (denominator + 1e-06)

        rs_copies = []
        ar_x = ar_z = ar_y = None
        everything = []
        for t in range(ITERS):
            arrived(ag_copies)
            everything += ag_copies
            for i in range(4):
                ag_two[h, pl.ds(i * NM, NM)] = split(ag[h, t, i])
            left(rs_copies)
            rs_copies = []
            for pair in range(4):
                rows = pl.ds(pair * 256, 256)
                rs_send[h, rows] = halves(dot(c_hi[rows], ag_two[h]) + dot(c_lo[rows], ag_two[h]))
                for k in (2 * pair, 2 * pair + 1):
                    if k < 7:
                        rs_copies.append(
                            send(rs_send.at[h, pl.ds(k * NM, NM)], rs_recv.at[h, t, back(*ZY[k])], zy_peer(*ZY[k]))
                        )
            if t > 0:
                ar_z = reduce_z(t - 1, ar_x)
                everything += ar_x
            yield
            arrived(rs_copies)
            total = rs_send[h, pl.ds(7 * NM, NM)]
            for k in range(7):
                total = total + rs_recv[h, t, k]
            corr_w[h, t, 0] = total
            corr_copies = [
                send(corr_w.at[h, t, 0], corr_w.at[h, t, 1], ring(1)),
                send(corr_w.at[h, t, 0], corr_w.at[h, t, 2], ring(-1)),
            ]
            if t > 0:
                ar_y = reduce_y(t - 1, ar_z)
                everything += ar_z
            yield
            if t > 0:
                alpha = reduced(t - 1, ar_y)
                everything += ar_y
            arrived(corr_copies)
            everything += corr_copies
            for i in range(3):
                value = corr_w[h, t, i]
                if t > 0:
                    value = corr[h, i] - alpha * value
                corr[h, i] = value
                corr_two[h, pl.ds(i * NM, NM)] = split(value)

            def make_direction(rows, base):
                columns = pl.ds(h * W, W)
                coarse_part = halves(dot(phi3_hi[rows], corr_two[h]) + dot(phi3_lo[rows], corr_two[h]))
                residual = r_out[rows, columns]
                if t > 0:
                    residual = residual - alpha * w_buf[h, rows]
                    r_out[rows, columns] = residual
                    step = alpha * d_buf[h, rows]
                    x_out[rows, columns] = step if t == 1 else x_out[rows, columns] + step
                value = delta[rows] * residual + coarse_part
                d_buf[h, rows] = value
                two[h, rows] = split(value)

            each_tile(ROW_TILES, TILE, make_direction)
            left(e_copies[t])

            def shared_product(rows, base):
                e_send[h, rows] = halves(dot(ss_hi[rows], two[h]) + dot(ss_lo[rows], two[h]))

            each_tile(2 * NS // TILE, TILE, shared_product)
            send_shared(t + 1)
            yield

            def product(rows, base):
                value = halves(dot(s_hi[rows], two[h]) + dot(s_lo[rows], two[h]))
                w_buf[h, rows] = jnp.where(live_mask(base, (TILE, W)), value, 0.0)

            each_tile(ROW_TILES, TILE, product)
            yield
            receive_shared(t + 1)

            def make_image(i, sums):
                base = i * TILE
                rows = pl.ds(pl.multiple_of(base, TILE), TILE)
                value = w_buf[h, rows] + scattered(rows)
                w_buf[h, rows] = value
                if t < ITERS - 1:
                    two[h, rows] = split(value)
                weighted = share[rows] * value
                return (
                    sums[0] + fold8(weighted * r_out[rows, pl.ds(h * W, W)]),
                    sums[1] + fold8(weighted * value),
                )

            numerator, denominator = lax.fori_loop(0, ROW_TILES, make_image, (zeros8(), zeros8()))
            ar_send[h, t, 0, pl.ds(0, 8)] = numerator
            ar_send[h, t, 0, pl.ds(8, 8)] = denominator
            ar_x = reduce_x(t)
            if t < ITERS - 1:
                ag_copies = modal_and_gather(t + 1)
            yield
        ar_z = reduce_z(ITERS - 1, ar_x)
        yield
        ar_y = reduce_y(ITERS - 1, ar_z)
        yield
        alpha = reduced(ITERS - 1, ar_y)

        def finish(rows, base):
            columns = pl.ds(h * W, W)
            r_out[rows, columns] = r_out[rows, columns] - alpha * w_buf[h, rows]
            x_out[rows, columns] = x_out[rows, columns] + alpha * d_buf[h, rows]

        each_tile(ROW_TILES, TILE, finish)
        left(everything + ar_x + ar_z + ar_y + rs_copies + e_copies[ITERS])
        yield

    streams = [stream(h) for h in range(STREAMS)]
    for one in streams:
        next(one)

    def build_rows(rows, base):
        local = lax.broadcasted_iota(jnp.int32, (TILE, 2 * NS), 0) + base
        hot = (local == index_row[...]).astype(F32)
        to_slots[rows] = hot.astype(BF16)
        counted = jnp.sum(hot, axis=1, keepdims=True)
        alive = jnp.where(live_mask(base, (TILE, 1)), 1.0, 0.0)
        share[rows] = jnp.broadcast_to(alive / (1.0 + counted), (TILE, W))

    each_tile(ROW_TILES, TILE, build_rows)

    def cut_chunk(i, carry):
        chunk_copy(i).wait()
        slot = lax.rem(i, 2)
        base = pl.multiple_of(i * CHUNK, CHUNK)
        rows = pl.ds(base, CHUNK)
        for part in range(7):
            columns = pl.ds(part * 256, 256)
            value = chunk[slot, :, columns]
            high = value.astype(BF16)
            s_hi[rows, columns] = high
            s_lo[rows, columns] = (value - high.astype(F32)).astype(BF16)
        block = chunk[slot, :, pl.ds(base, CHUNK)]
        same = lax.broadcasted_iota(jnp.int32, (CHUNK, CHUNK), 0) == lax.broadcasted_iota(
            jnp.int32, (CHUNK, CHUNK), 1
        )
        diagonal = jnp.sum(jnp.where(same, block, 0.0), axis=1, keepdims=True)
        delta[rows] = share[rows] / diagonal
        return carry

    def cut_and_next(i, carry):
        cut_chunk(i, carry)
        chunk_copy(i + 2).start()
        return carry

    lax.fori_loop(0, CHUNKS - 2, cut_and_next, 0)
    lax.fori_loop(CHUNKS - 2, CHUNKS, cut_chunk, 0)

    loads[STREAMS].wait()
    mode_mask = lax.broadcasted_iota(jnp.int32, (TILE, NM), 1) < modes_live

    def weigh_modes(rows, base):
        value = jnp.where(mode_mask, share[rows] * phi[rows], 0.0)
        both = split(value)
        phi3_hi[rows, pl.ds(0, NM)] = both[:, :NM]
        phi3_lo[rows, pl.ds(0, NM)] = both[:, NM:]
        phit_hi[:, rows] = value.T.astype(BF16)
        phit_lo[:, rows] = both[:, NM:].astype(F32).T.astype(BF16)
        two[STREAMS, rows] = split(delta[rows])

    each_tile(ROW_TILES, TILE, weigh_modes)

    def gather_pair(rows, base):
        hot = from_slots[rows]
        pair_send[rows, pl.ds(0, NM)] = dot(hot, phi3_hi[:, pl.ds(0, NM)]) + dot(hot, phi3_lo[:, pl.ds(0, NM)])
        pair_send[rows, pl.ds(NM, NM)] = halves(dot(hot, two[STREAMS]))

    each_tile(2 * NS // TILE, TILE, gather_pair)
    pair_copies = exchange(pair_send, pair_recv)

    for one in streams:
        next(one)

    def gather_schur(rows, base):
        hot = from_slots[rows]
        for part in range(7):
            columns = pl.ds(part * 256, 256)
            ss_hi[rows, columns] = dot(hot, s_hi[:, columns]).astype(BF16)
            ss_lo[rows, columns] = dot(hot, s_lo[:, columns]).astype(BF16)

    each_tile(2 * NS // TILE, TILE, gather_schur)

    loads[STREAMS + 1].wait()
    arrived(c_copies)
    for k in range(8):
        both = split(c_in[k])
        c_hi[pl.ds(k * NM, NM)] = both[:, :512]
        c_lo[pl.ds(k * NM, NM)] = both[:, 512:]

    for one in streams:
        next(one)

    arrived(pair_copies)

    def cut_pair(rows, base):
        value = pair_recv[rows]
        high = value.astype(BF16)
        two[STREAMS, rows] = high
        pair_send_low[rows] = (value - high.astype(F32)).astype(BF16)

    pair_send_low = two.at[STREAMS + 1]
    each_tile(2 * NS // TILE, TILE, cut_pair)

    def place_pair(rows, base):
        for side in range(2):
            slots = pl.ds(side * NS, NS)
            hot = to_slots[rows, slots]
            high = dot(hot, two[STREAMS, slots])
            low = dot(hot, pair_send_low[slots])
            columns = pl.ds((1 + side) * NM, NM)
            phi3_hi[rows, columns] = high[:, :NM].astype(BF16)
            phi3_lo[rows, columns] = low[:, :NM].astype(BF16)
            delta[rows] = delta[rows] + (high[:, NM:] + low[:, NM:])

    each_tile(ROW_TILES, TILE, place_pair)

    running = True
    while running:
        for one in streams:
            if next(one, None) is None and one.gi_frame is None:
                running = False
    left(c_copies)
    left(pair_copies)


def local(load, schur, modes, coarse_inverse, interface_rows, mode_count, left_rows, right_rows):
    index_row = jnp.concatenate([left_rows, right_rows], axis=1)
    index_column = index_row.reshape(2 * NS, 1)
    vmem = pl.BlockSpec(memory_space=pltpu.VMEM)
    smem = pl.BlockSpec(memory_space=pltpu.SMEM)
    anywhere = pl.BlockSpec(memory_space=pl.ANY)
    copies = 7 + 2 + STREAMS * (2 * (ITERS + 1) + ITERS * (3 + 7 + 2 + 3 + 3 + 7))
    return pl.pallas_call(
        kernel,
        out_shape=(jax.ShapeDtypeStruct((NI, K), F32), jax.ShapeDtypeStruct((NI, K), F32)),
        in_specs=[anywhere, anywhere, anywhere, anywhere, smem, smem, vmem, vmem],
        out_specs=(vmem, vmem),
        scratch_shapes=[
            pltpu.VMEM((NI, NI), BF16),
            pltpu.VMEM((NI, NI), BF16),
            pltpu.VMEM((2 * NS, NI), BF16),
            pltpu.VMEM((2 * NS, NI), BF16),
            pltpu.VMEM((2, CHUNK, NI), F32),
            pltpu.VMEM((NI, 2 * NS), BF16),
            pltpu.VMEM((2 * NS, NI), BF16),
            pltpu.VMEM((NI, NM), F32),
            pltpu.VMEM((NM, NI), BF16),
            pltpu.VMEM((NM, NI), BF16),
            pltpu.VMEM((NI, 3 * NM), BF16),
            pltpu.VMEM((NI, 3 * NM), BF16),
            pltpu.VMEM((8, NM, 512), F32),
            pltpu.VMEM((8 * NM, 512), BF16),
            pltpu.VMEM((8 * NM, 512), BF16),
            pltpu.VMEM((NI, W), F32),
            pltpu.VMEM((NI, W), F32),
            pltpu.VMEM((2 * NS, 2 * NM), F32),
            pltpu.VMEM((2 * NS, 2 * NM), F32),
            pltpu.VMEM((STREAMS, NI, W), F32),
            pltpu.VMEM((STREAMS, NI, W), F32),
            pltpu.VMEM((STREAMS + 2, NI, 2 * W), BF16),
            pltpu.VMEM((STREAMS, 2 * NS, W), F32),
            pltpu.VMEM((STREAMS, ITERS + 1, 2 * NS, W), F32),
            pltpu.VMEM((STREAMS, ITERS, 4, NM, W), F32),
            pltpu.VMEM((STREAMS, 4 * NM, 2 * W), BF16),
            pltpu.VMEM((STREAMS, 8 * NM, W), F32),
            pltpu.VMEM((STREAMS, ITERS, 7, NM, W), F32),
            pltpu.VMEM((STREAMS, 3, NM, W), F32),
            pltpu.VMEM((STREAMS, ITERS, 3, NM, W), F32),
            pltpu.VMEM((STREAMS, 3 * NM, 2 * W), BF16),
            pltpu.VMEM((STREAMS, ITERS, 3, 16, W), F32),
            pltpu.VMEM((STREAMS, ITERS, 13, 16, W), F32),
            pltpu.SemaphoreType.DMA((STREAMS + 2,)),
            pltpu.SemaphoreType.DMA((2,)),
            pltpu.SemaphoreType.DMA((copies,)),
            pltpu.SemaphoreType.DMA((copies,)),
        ],
        compiler_params=pltpu.CompilerParams(
            collective_id=0, has_side_effects=True, vmem_limit_bytes=62 * 1024 * 1024
        ),
        cost_estimate=pl.CostEstimate(flops=20 * 10**9, bytes_accessed=21 * 10**6, transcendentals=0),
    )(load, schur, modes, coarse_inverse, interface_rows, mode_count, index_row, index_column)


def solution(mesh):
    return jax.shard_map(
        local,
        mesh=mesh,
        in_specs=(
            P(("cluster", "sub"), None),
            P(("cluster", "sub"), None),
            P(("cluster", "sub"), None),
            P(("cluster", "sub"), None),
            P(("cluster", "sub")),
            P(("cluster", "sub")),
            P(("cluster", "sub"), None),
            P(("cluster", "sub"), None),
        ),
        out_specs=(P(("cluster", "sub"), None), P(("cluster", "sub"), None)),
        check_vma=False,
    )
```

```python
import functools

import jax
import jax.numpy as jnp
from jax import lax
from jax.experimental import pallas as pl
from jax.experimental.pallas import tpu as pltpu
from jax.sharding import PartitionSpec as P

MESH = pl.DeviceIdType.MESH
F32 = jnp.float32
BF16 = jnp.bfloat16
NI = 1792
NS = 384
K = 256
NM = 128
ITERS = 3
W = 128
STREAMS = K // W
TILE = 448
ROW_TILES = NI // TILE
CHUNK = 128
CHUNKS = NI // CHUNK
BUFFERS = 4

ZY = [(2, 1), (2, 0), (1, 1), (3, 1), (1, 0), (3, 0), (0, 1), (0, 0)]
YC = [(dy, dc) for dy in (2, 1, 3, 0) for dc in (1, 0) if (dy, dc) != (0, 0)]
THREE = (2, 1, 3)


def split(value):
    high = value.astype(BF16)
    low = (value - high.astype(F32)).astype(BF16)
    return jnp.concatenate([high, low], axis=1)


def halves(value):
    width = value.shape[1] // 2
    return value[:, :width] + value[:, width:]


def dot(a, b):
    return jnp.dot(a, b, preferred_element_type=F32)


def each_tile(count, size, body):
    def step(i, carry):
        body(pl.ds(pl.multiple_of(i * size, size), size), i * size)
        return carry

    lax.fori_loop(0, count, step, 0)


def kernel(
    load, schur, modes, coarse, live_rows, mode_count, left_rows, right_rows,
    x_out, r_out,
    s_hi, s_lo, chunk, to_slots, from_slots, phi, phit_hi, phit_lo, phi3_hi, phi3_lo, b_hi, b_lo,
    c_in, c_hi, c_lo, share, delta, pair_send, pair_recv,
    w_buf, scaled_hi, scaled_lo, smooth, smooth_w, two, e_two, e_send, e_recv, ag, ag_two, rs_send, rs_recv,
    corr, corr_w, corr_sum, corr_two, sum_two, ar_send, ar_recv,
    local_sem, chunk_sem, send_sem, recv_sem,
):
    c = lax.axis_index("cluster")
    s = lax.axis_index("sub")
    z, yh, xx = s // 8, (s // 4) % 2, s % 4
    g = c * 32 + s

    def ring(by):
        t = (g + by + 128) % 128
        return (t // 32, t % 32)

    def x_peer(dx):
        return (c, z * 8 + yh * 4 + (xx + dx) % 4)

    def zy_line(dz, dy):
        return ((z + dz) % 4) * 2 + (yh + dy) % 2

    def zy_peer(dz, dy):
        return (c, zy_line(dz, dy) * 4 + xx)

    def yc_peer(dy, dc):
        y = (yh * 2 + c // 2 + dy) % 4
        return ((y % 2) * 2 + (c + dc) % 2, z * 8 + (y // 2) * 4 + xx)

    def back(dz, dy):
        return ZY.index(((4 - dz) % 4, (2 - dy) % 2))

    counter = [0]

    def send(src, dst, peer):
        n = counter[0]
        counter[0] = n + 1
        copy = pltpu.make_async_remote_copy(
            src_ref=src, dst_ref=dst, send_sem=send_sem.at[n], recv_sem=recv_sem.at[n],
            device_id=peer, device_id_type=MESH,
        )
        copy.start()
        return copy

    loads = [
        pltpu.make_async_copy(load.at[:, pl.ds(h * W, W)], w_buf.at[h], local_sem.at[h])
        for h in range(STREAMS)
    ]
    loads.append(pltpu.make_async_copy(modes, phi, local_sem.at[STREAMS]))
    line = z * 2 + yh
    loads.append(
        pltpu.make_async_copy(
            coarse.at[:, pl.ds(pl.multiple_of(line * 512, 512), 512)], c_in.at[7], local_sem.at[STREAMS + 1]
        )
    )
    for copy in loads:
        copy.start()

    def chunk_copy(i):
        slot = lax.rem(i, BUFFERS)
        return pltpu.make_async_copy(
            schur.at[pl.ds(pl.multiple_of(i * CHUNK, CHUNK), CHUNK)], chunk.at[slot], chunk_sem.at[slot]
        )

    for i in range(BUFFERS):
        chunk_copy(i).start()

    peers = [ring(1), ring(-1)]
    peers += [x_peer(d) for d in THREE]
    peers += [zy_peer(*d) for d in ZY[:-1]]
    peers += [yc_peer(*d) for d in YC]
    barrier = pltpu.get_barrier_semaphore()
    for peer in peers:
        pl.semaphore_signal(barrier, inc=1, device_id=peer, device_id_type=MESH)

    live_count = live_rows[0]
    modes_live = mode_count[0]
    sides = (left_rows, right_rows)

    for side in range(2):
        column = jnp.broadcast_to(sides[side][...].astype(F32), (128, NS)).T
        lanes = lax.broadcasted_iota(jnp.int32, (NS, 128), 1).astype(F32)
        for part in range(NI // 128):
            hot = jnp.where(lanes + float(part * 128) == column, 1.0, 0.0)
            from_slots[pl.ds(side * NS, NS), pl.ds(part * 128, 128)] = hot.astype(BF16)

    def live_mask(base, shape):
        return (lax.broadcasted_iota(jnp.int32, shape, 0) + base) < live_count

    for h in range(STREAMS):
        loads[h].wait()

        def mask_load(rows, base, h=h):
            value = jnp.where(live_mask(base, (TILE, W)), w_buf[h, rows], 0.0)
            w_buf[h, rows] = value
            two[h, rows] = split(value)

        each_tile(ROW_TILES, TILE, mask_load)

    pl.semaphore_wait(barrier, len(peers))

    def exchange(src, dst):
        return [
            send(src.at[pl.ds(NS, NS)], dst.at[pl.ds(0, NS)], ring(1)),
            send(src.at[pl.ds(0, NS)], dst.at[pl.ds(NS, NS)], ring(-1)),
        ]

    def arrived(copies):
        for copy in copies:
            copy.wait_recv()

    def left(copies):
        for copy in copies:
            copy.wait_send()

    def stream(h):
        columns = pl.ds(h * W, W)
        e_copies = []
        everything = []

        def send_shared(t):
            def gather(rows, base):
                e_send[h, rows] = halves(dot(from_slots[rows], two[h]))

            each_tile(2, NS, gather)
            e_copies.append(exchange(e_send.at[h], e_recv.at[h, t]))

        def receive_shared(t):
            arrived(e_copies[t])

            def cut(rows, base):
                e_two[rows] = split(e_recv[h, t, rows])

            each_tile(2, NS, cut)

        def scattered(rows):
            return halves(dot(to_slots[rows], e_two[...]))

        def modal_and_gather(t):
            modal = halves(dot(phit_hi[...], two[h]) + dot(phit_lo[...], two[h]))
            ag[h, t, xx] = modal
            return [send(ag.at[h, t, xx], ag.at[h, t, xx], x_peer(d)) for d in THREE]

        def reduce_x(t):
            return [send(ar_send.at[h, t, 0], ar_recv.at[h, t, i], x_peer(d)) for i, d in enumerate(THREE)]

        def reduce_z(t, copies):
            arrived(copies)
            ar_send[h, t, 1] = ar_send[h, t, 0] + ar_recv[h, t, 0] + ar_recv[h, t, 1] + ar_recv[h, t, 2]
            return [send(ar_send.at[h, t, 1], ar_recv.at[h, t, 3 + i], zy_peer(d, 0)) for i, d in enumerate(THREE)]

        def reduce_y(t, copies):
            arrived(copies)
            ar_send[h, t, 2] = ar_send[h, t, 1] + ar_recv[h, t, 3] + ar_recv[h, t, 4] + ar_recv[h, t, 5]
            return [send(ar_send.at[h, t, 2], ar_recv.at[h, t, 6 + i], yc_peer(*d)) for i, d in enumerate(YC)]

        def reduced(t, copies):
            arrived(copies)
            total = ar_send[h, t, 2]
            for i in range(7):
                total = total + ar_recv[h, t, 6 + i]
            numerator = jnp.sum(total[:8], axis=0, keepdims=True)
            denominator = jnp.sum(total[8:], axis=0, keepdims=True)
            return numerator / (denominator + 1e-06)

        send_shared(0)
        yield
        receive_shared(0)

        def first_residual(rows, base):
            value = w_buf[h, rows] + scattered(rows)
            r_out[rows, columns] = value
            two[h, rows] = split(value)

        each_tile(ROW_TILES, TILE, first_residual)
        ag_copies = modal_and_gather(0)
        yield

        rs_copies = []
        ar_x = ar_z = ar_y = None
        for t in range(ITERS):
            arrived(ag_copies)
            everything += ag_copies
            for i in range(4):
                ag_two[h, pl.ds(i * NM, NM)] = split(ag[h, t, i])
            left(rs_copies)
            rs_copies = []
            for pair in range(4):
                rows = pl.ds(pair * 256, 256)
                rs_send[h, rows] = halves(dot(c_hi[rows], ag_two[h]) + dot(c_lo[rows], ag_two[h]))
                for k in (2 * pair, 2 * pair + 1):
                    if k < 7:
                        rs_copies.append(
                            send(rs_send.at[h, pl.ds(k * NM, NM)], rs_recv.at[h, t, back(*ZY[k])], zy_peer(*ZY[k]))
                        )
            if t > 0:
                ar_z = reduce_z(t - 1, ar_x)
                everything += ar_x
            yield
            arrived(rs_copies)
            total = rs_send[h, pl.ds(7 * NM, NM)]
            for k in range(7):
                total = total + rs_recv[h, t, k]
            corr_w[h, t, 0] = total
            corr_copies = [
                send(corr_w.at[h, t, 0], corr_w.at[h, t, 1], ring(1)),
                send(corr_w.at[h, t, 0], corr_w.at[h, t, 2], ring(-1)),
            ]
            if t > 0:
                ar_y = reduce_y(t - 1, ar_z)
                everything += ar_z
            yield
            if t > 0:
                alpha = reduced(t - 1, ar_y)
                everything += ar_y
            arrived(corr_copies)
            everything += corr_copies
            for i in range(3):
                value = corr_w[h, t, i]
                if t > 0:
                    step = alpha * corr[h, i]
                    corr_sum[h, i] = step if t == 1 else corr_sum[h, i] + step
                    value = corr[h, i] - alpha * value
                corr[h, i] = value
                corr_two[h, pl.ds(i * NM, NM)] = split(value)

            def make_product(rows, base):
                value = smooth[rows, columns]
                if t > 0:
                    value = value - alpha * smooth_w[rows, columns]
                    smooth[rows, columns] = value
                    residual = r_out[rows, columns]
                    step = alpha * residual
                    x_out[rows, columns] = step if t == 1 else x_out[rows, columns] + step
                    r_out[rows, columns] = residual - alpha * w_buf[h, rows]
                value = value + halves(dot(b_hi[rows], corr_two[h]) + dot(b_lo[rows], corr_two[h]))
                value = jnp.where(live_mask(base, (TILE, W)), value, 0.0)
                w_buf[h, rows] = value
                two[h, rows] = split(value)

            each_tile(ROW_TILES, TILE, make_product)
            left(e_copies[t])
            send_shared(t + 1)
            yield
            receive_shared(t + 1)

            def make_image(i, sums):
                base = i * TILE
                rows = pl.ds(pl.multiple_of(base, TILE), TILE)
                value = w_buf[h, rows] + scattered(rows)
                w_buf[h, rows] = value
                if t < ITERS - 1:
                    two[h, rows] = split(value)
                    both = split(delta[rows] * value)
                    scaled_hi[rows, columns] = both[:, :W]
                    scaled_lo[rows, columns] = both[:, W:]
                weighted = share[rows] * value
                fold = lambda v: jnp.sum(v.reshape(TILE // 8, 8, W), axis=0)
                return (
                    sums[0] + fold(weighted * r_out[rows, columns]),
                    sums[1] + fold(weighted * value),
                )

            nothing = jnp.zeros((8, W), F32)
            numerator, denominator = lax.fori_loop(0, ROW_TILES, make_image, (nothing, nothing))
            ar_send[h, t, 0, pl.ds(0, 8)] = numerator
            ar_send[h, t, 0, pl.ds(8, 8)] = denominator
            ar_x = reduce_x(t)
            if t < ITERS - 1:
                ag_copies = modal_and_gather(t + 1)
            yield
        ar_z = reduce_z(ITERS - 1, ar_x)
        yield
        ar_y = reduce_y(ITERS - 1, ar_z)
        yield
        alpha = reduced(ITERS - 1, ar_y)

        def finish(rows, base):
            r_out[rows, columns] = r_out[rows, columns] - alpha * w_buf[h, rows]
            x_out[rows, columns] = x_out[rows, columns] + alpha * smooth_w[rows, columns]

        each_tile(ROW_TILES, TILE, finish)
        left(everything + ar_x + ar_z + ar_y + rs_copies + e_copies[ITERS])
        yield

    streams = [stream(h) for h in range(STREAMS)]

    def advance():
        for one in streams:
            next(one)

    advance()
    c_copies = [
        send(
            coarse.at[:, pl.ds(pl.multiple_of(zy_line(dz, dy) * 512, 512), 512)],
            c_in.at[back(dz, dy)],
            zy_peer(dz, dy),
        )
        for dz, dy in ZY[:-1]
    ]

    def build_rows(rows, base):
        local = lax.broadcasted_iota(jnp.int32, (TILE, NS), 0) + base
        counted = jnp.zeros((TILE, 1), F32)
        for side in range(2):
            hot = jnp.where(local == sides[side][...], 1.0, 0.0)
            to_slots[rows, pl.ds(side * NS, NS)] = hot.astype(BF16)
            counted = counted + jnp.sum(hot, axis=1, keepdims=True)
        alive = jnp.where(live_mask(base, (TILE, 1)), 1.0, 0.0)
        share[rows] = jnp.broadcast_to(alive / (1.0 + counted), (TILE, W))

    each_tile(ROW_TILES, TILE, build_rows)

    def cut_chunk(i, carry):
        chunk_copy(i).wait()
        slot = lax.rem(i, BUFFERS)
        base = pl.multiple_of(i * CHUNK, CHUNK)
        rows = pl.ds(base, CHUNK)
        for part in range(7):
            columns = pl.ds(part * 256, 256)
            value = chunk[slot, :, columns]
            high = value.astype(BF16)
            s_hi[rows, columns] = high
            s_lo[rows, columns] = (value - high.astype(F32)).astype(BF16)
        block = chunk[slot, :, pl.ds(base, CHUNK)]
        same = lax.broadcasted_iota(jnp.int32, (CHUNK, CHUNK), 0) == lax.broadcasted_iota(
            jnp.int32, (CHUNK, CHUNK), 1
        )
        diagonal = jnp.sum(jnp.where(same, block, 0.0), axis=1, keepdims=True)
        delta[rows] = share[rows] / diagonal
        return carry

    def cut_and_next(i, carry):
        cut_chunk(i, carry)
        chunk_copy(i + BUFFERS).start()
        return carry

    lax.fori_loop(0, CHUNKS - BUFFERS, cut_and_next, 0)
    lax.fori_loop(CHUNKS - BUFFERS, CHUNKS, cut_chunk, 0)

    loads[STREAMS].wait()
    mode_mask = lax.broadcasted_iota(jnp.int32, (256, NM), 1) < modes_live

    def weigh_modes(rows, base):
        value = jnp.where(mode_mask, share[rows] * phi[rows], 0.0)
        both = split(value)
        phi3_hi[rows, pl.ds(0, NM)] = both[:, :NM]
        phi3_lo[rows, pl.ds(0, NM)] = both[:, NM:]
        turned = value.T
        high = turned.astype(BF16)
        phit_hi[:, rows] = high
        phit_lo[:, rows] = (turned - high.astype(F32)).astype(BF16)
        scale = split(delta[rows])
        scaled_hi[rows] = jnp.concatenate([both[:, :NM], scale[:, :NM]], axis=1)
        scaled_lo[rows] = jnp.concatenate([both[:, NM:], scale[:, NM:]], axis=1)

    each_tile(7, 256, weigh_modes)

    def gather_pair(rows, base):
        hot = from_slots[rows]
        pair_send[rows] = dot(hot, scaled_hi[...]) + dot(hot, scaled_lo[...])

    each_tile(2, NS, gather_pair)
    pair_copies = exchange(pair_send, pair_recv)

    advance()
    loads[STREAMS + 1].wait()
    arrived(c_copies)
    for k in range(8):
        both = split(c_in[k])
        c_hi[pl.ds(k * NM, NM)] = both[:, :512]
        c_lo[pl.ds(k * NM, NM)] = both[:, 512:]

    arrived(pair_copies)

    def cut_pair(rows, base):
        value = pair_recv[rows]
        high = value.astype(BF16)
        scaled_hi[rows] = high
        scaled_lo[rows] = (value - high.astype(F32)).astype(BF16)

    each_tile(2, NS, cut_pair)

    def place_pair(rows, base):
        for side in range(2):
            slots = pl.ds(side * NS, NS)
            hot = to_slots[rows, slots]
            high = dot(hot, scaled_hi[slots])
            low = dot(hot, scaled_lo[slots])
            columns = pl.ds((1 + side) * NM, NM)
            phi3_hi[rows, columns] = high[:, :NM].astype(BF16)
            phi3_lo[rows, columns] = low[:, :NM].astype(BF16)
            delta[rows] = delta[rows] + (high[:, NM:] + low[:, NM:])

    each_tile(ROW_TILES, TILE, place_pair)

    def scale_residual(rows, base):
        for h in range(STREAMS):
            columns = pl.ds(h * W, W)
            both = split(delta[rows] * r_out[rows, columns])
            scaled_hi[rows, columns] = both[:, :W]
            scaled_lo[rows, columns] = both[:, W:]

    each_tile(ROW_TILES, TILE, scale_residual)

    def smoother(target, first, last):
        def tile(i, carry):
            rows = pl.ds(pl.multiple_of(i * TILE, TILE), TILE)
            target[rows] = (
                dot(s_hi[rows], scaled_hi[...]) + dot(s_hi[rows], scaled_lo[...]) + dot(s_lo[rows], scaled_hi[...])
            )
            return carry

        lax.fori_loop(first, last, tile, 0)

    def schur_modes(first, last):
        def tile(i, carry):
            rows = pl.ds(pl.multiple_of(i * TILE, TILE), TILE)
            value = dot(s_hi[rows], phi3_hi[...]) + dot(s_hi[rows], phi3_lo[...]) + dot(s_lo[rows], phi3_hi[...])
            high = value.astype(BF16)
            b_hi[rows] = high
            b_lo[rows] = (value - high.astype(F32)).astype(BF16)
            return carry

        lax.fori_loop(first, last, tile, 0)

    smoother(smooth, 0, 2)
    advance()
    smoother(smooth, 2, 4)
    schur_modes(0, 2)
    advance()
    schur_modes(2, 4)
    advance()
    for t in range(1, ITERS):
        advance()
        smoother(smooth_w, 0, 1)
        advance()
        smoother(smooth_w, 1, 3)
        advance()
        smoother(smooth_w, 3, 4)
        advance()

    for h in range(STREAMS):
        columns = pl.ds(h * W, W)
        for i in range(3):
            sum_two[pl.ds(i * NM, NM)] = split(corr_sum[h, i])

        def prolong(rows, base):
            high, low = phi3_hi[rows], phi3_lo[rows]
            x_out[rows, columns] = delta[rows] * x_out[rows, columns] + halves(
                dot(high, sum_two[...]) + dot(low, sum_two[...])
            )
            smooth_w[rows, columns] = delta[rows] * r_out[rows, columns] + halves(
                dot(high, corr_two[h]) + dot(low, corr_two[h])
            )

        each_tile(ROW_TILES, TILE, prolong)
    for _ in range(4):
        advance()
    left(c_copies)
    left(pair_copies)


def local(load, schur, modes, coarse_inverse, interface_rows, mode_count, left_rows, right_rows):
    vmem = pl.BlockSpec(memory_space=pltpu.VMEM)
    smem = pl.BlockSpec(memory_space=pltpu.SMEM)
    anywhere = pl.BlockSpec(memory_space=pl.ANY)
    copies = 7 + 2 + STREAMS * (2 * (ITERS + 1) + ITERS * (3 + 7 + 2 + 3 + 3 + 7))
    return pl.pallas_call(
        kernel,
        out_shape=(jax.ShapeDtypeStruct((NI, K), F32), jax.ShapeDtypeStruct((NI, K), F32)),
        in_specs=[anywhere, anywhere, anywhere, anywhere, smem, smem, vmem, vmem],
        out_specs=(vmem, vmem),
        scratch_shapes=[
            pltpu.VMEM((NI, NI), BF16),
            pltpu.VMEM((NI, NI), BF16),
            pltpu.VMEM((BUFFERS, CHUNK, NI), F32),
            pltpu.VMEM((NI, 2 * NS), BF16),
            pltpu.VMEM((2 * NS, NI), BF16),
            pltpu.VMEM((NI, NM), F32),
            pltpu.VMEM((NM, NI), BF16),
            pltpu.VMEM((NM, NI), BF16),
            pltpu.VMEM((NI, 3 * NM), BF16),
            pltpu.VMEM((NI, 3 * NM), BF16),
            pltpu.VMEM((NI, 3 * NM), BF16),
            pltpu.VMEM((NI, 3 * NM), BF16),
            pltpu.VMEM((8, NM, 512), F32),
            pltpu.VMEM((8 * NM, 512), BF16),
            pltpu.VMEM((8 * NM, 512), BF16),
            pltpu.VMEM((NI, W), F32),
            pltpu.VMEM((NI, W), F32),
            pltpu.VMEM((2 * NS, 2 * NM), F32),
            pltpu.VMEM((2 * NS, 2 * NM), F32),
            pltpu.VMEM((STREAMS, NI, W), F32),
            pltpu.VMEM((NI, K), BF16),
            pltpu.VMEM((NI, K), BF16),
            pltpu.VMEM((NI, K), F32),
            pltpu.VMEM((NI, K), F32),
            pltpu.VMEM((STREAMS, NI, 2 * W), BF16),
            pltpu.VMEM((2 * NS, 2 * W), BF16),
            pltpu.VMEM((STREAMS, 2 * NS, W), F32),
            pltpu.VMEM((STREAMS, ITERS + 1, 2 * NS, W), F32),
            pltpu.VMEM((STREAMS, ITERS, 4, NM, W), F32),
            pltpu.VMEM((STREAMS, 4 * NM, 2 * W), BF16),
            pltpu.VMEM((STREAMS, 8 * NM, W), F32),
            pltpu.VMEM((STREAMS, ITERS, 7, NM, W), F32),
            pltpu.VMEM((STREAMS, 3, NM, W), F32),
            pltpu.VMEM((STREAMS, ITERS, 3, NM, W), F32),
            pltpu.VMEM((STREAMS, 3, NM, W), F32),
            pltpu.VMEM((STREAMS, 3 * NM, 2 * W), BF16),
            pltpu.VMEM((3 * NM, 2 * W), BF16),
            pltpu.VMEM((STREAMS, ITERS, 3, 16, W), F32),
            pltpu.VMEM((STREAMS, ITERS, 13, 16, W), F32),
            pltpu.SemaphoreType.DMA((STREAMS + 2,)),
            pltpu.SemaphoreType.DMA((BUFFERS,)),
            pltpu.SemaphoreType.DMA((copies,)),
            pltpu.SemaphoreType.DMA((copies,)),
        ],
        compiler_params=pltpu.CompilerParams(
            collective_id=0, has_side_effects=True, vmem_limit_bytes=62 * 1024 * 1024
        ),
        cost_estimate=pl.CostEstimate(flops=20 * 10**9, bytes_accessed=21 * 10**6, transcendentals=0),
    )(load, schur, modes, coarse_inverse, interface_rows, mode_count, left_rows, right_rows)


def solution(mesh):
    return jax.shard_map(
        local,
        mesh=mesh,
        in_specs=(
            P(("cluster", "sub"), None),
            P(("cluster", "sub"), None),
            P(("cluster", "sub"), None),
            P(("cluster", "sub"), None),
            P(("cluster", "sub")),
            P(("cluster", "sub")),
            P(("cluster", "sub"), None),
            P(("cluster", "sub"), None),
        ),
        out_specs=(P(("cluster", "sub"), None), P(("cluster", "sub"), None)),
        check_vma=False,
    )
```

```python
import functools

import jax
import jax.numpy as jnp
from jax import lax
from jax.experimental import pallas as pl
from jax.experimental.pallas import tpu as pltpu
from jax.sharding import PartitionSpec as P

MESH = pl.DeviceIdType.MESH
F32 = jnp.float32
BF16 = jnp.bfloat16
NI = 1792
NS = 384
K = 256
NM = 128
ITERS = 3
W = 128
STREAMS = K // W
TILE = 448
ROW_TILES = NI // TILE
CHUNK = 128
CHUNKS = NI // CHUNK
BUFFERS = 4

ZY = [(2, 1), (2, 0), (1, 1), (3, 1), (1, 0), (3, 0), (0, 1), (0, 0)]
YC = [(dy, dc) for dy in (2, 1, 3, 0) for dc in (1, 0) if (dy, dc) != (0, 0)]
THREE = (2, 1, 3)


def split(value):
    high = value.astype(BF16)
    low = (value - high.astype(F32)).astype(BF16)
    return jnp.concatenate([high, low], axis=1)


def halves(value):
    width = value.shape[1] // 2
    return value[:, :width] + value[:, width:]


def dot(a, b):
    return jnp.dot(a, b, preferred_element_type=F32)


def each_tile(count, size, body):
    def step(i, carry):
        body(pl.ds(pl.multiple_of(i * size, size), size), i * size)
        return carry

    lax.fori_loop(0, count, step, 0)


def kernel(
    load, schur, modes, coarse, live_rows, mode_count, left_rows, right_rows,
    x_out, r_out,
    s_hi, s_lo, chunk, to_slots, from_slots, phi, phit_hi, phit_lo, phi3, b_hi, b_lo,
    c_in, c_hi, c_lo, share, delta, pair_send, pair_recv,
    w_buf, scaled_hi, scaled_lo, smooth, smooth_w, two, e_two, e_send, e_recv, ag, ag_two, rs_send, rs_recv,
    corr, corr_w, corr_sum, corr_two, sum_two, ar_send, ar_recv,
    local_sem, chunk_sem, send_sem, recv_sem,
):
    c = lax.axis_index("cluster")
    s = lax.axis_index("sub")
    z, yh, xx = s // 8, (s // 4) % 2, s % 4
    g = c * 32 + s

    def ring(by):
        t = (g + by + 128) % 128
        return (t // 32, t % 32)

    def x_peer(dx):
        return (c, z * 8 + yh * 4 + (xx + dx) % 4)

    def zy_line(dz, dy):
        return ((z + dz) % 4) * 2 + (yh + dy) % 2

    def zy_peer(dz, dy):
        return (c, zy_line(dz, dy) * 4 + xx)

    def yc_peer(dy, dc):
        y = (yh * 2 + c // 2 + dy) % 4
        return ((y % 2) * 2 + (c + dc) % 2, z * 8 + (y // 2) * 4 + xx)

    def back(dz, dy):
        return ZY.index(((4 - dz) % 4, (2 - dy) % 2))

    phi3_hi = phi3.at[:, pl.ds(0, 3 * NM)]
    phi3_lo = phi3.at[:, pl.ds(3 * NM, 3 * NM)]
    counter = [0]

    def send(src, dst, peer):
        n = counter[0]
        counter[0] = n + 1
        copy = pltpu.make_async_remote_copy(
            src_ref=src, dst_ref=dst, send_sem=send_sem.at[n], recv_sem=recv_sem.at[n],
            device_id=peer, device_id_type=MESH,
        )
        copy.start()
        return copy

    loads = [
        pltpu.make_async_copy(load.at[:, pl.ds(h * W, W)], w_buf.at[h], local_sem.at[h])
        for h in range(STREAMS)
    ]
    loads.append(pltpu.make_async_copy(modes, phi, local_sem.at[STREAMS]))
    line = z * 2 + yh
    loads.append(
        pltpu.make_async_copy(
            coarse.at[:, pl.ds(pl.multiple_of(line * 512, 512), 512)], c_in.at[7], local_sem.at[STREAMS + 1]
        )
    )
    for copy in loads:
        copy.start()

    def chunk_copy(i):
        slot = lax.rem(i, BUFFERS)
        return pltpu.make_async_copy(
            schur.at[pl.ds(pl.multiple_of(i * CHUNK, CHUNK), CHUNK)], chunk.at[slot], chunk_sem.at[slot]
        )

    for i in range(BUFFERS):
        chunk_copy(i).start()

    peers = [ring(1), ring(-1)]
    peers += [x_peer(d) for d in THREE]
    peers += [zy_peer(*d) for d in ZY[:-1]]
    peers += [yc_peer(*d) for d in YC]
    barrier = pltpu.get_barrier_semaphore()
    for peer in peers:
        pl.semaphore_signal(barrier, inc=1, device_id=peer, device_id_type=MESH)

    live_count = live_rows[0]
    modes_live = mode_count[0]
    sides = (left_rows, right_rows)

    for side in range(2):
        column = jnp.broadcast_to(sides[side][...].astype(F32), (128, NS)).T
        lanes = lax.broadcasted_iota(jnp.int32, (NS, 128), 1).astype(F32)
        for part in range(NI // 128):
            hot = jnp.where(lanes + float(part * 128) == column, 1.0, 0.0)
            from_slots[pl.ds(side * NS, NS), pl.ds(part * 128, 128)] = hot.astype(BF16)

    def live_mask(base, shape):
        return (lax.broadcasted_iota(jnp.int32, shape, 0) + base) < live_count

    for h in range(STREAMS):
        loads[h].wait()

        def mask_load(rows, base, h=h):
            value = jnp.where(live_mask(base, (TILE, W)), w_buf[h, rows], 0.0)
            w_buf[h, rows] = value
            two[h, rows] = split(value)

        each_tile(ROW_TILES, TILE, mask_load)

    pl.semaphore_wait(barrier, len(peers))

    def exchange(src, dst):
        return [
            send(src.at[pl.ds(NS, NS)], dst.at[pl.ds(0, NS)], ring(1)),
            send(src.at[pl.ds(0, NS)], dst.at[pl.ds(NS, NS)], ring(-1)),
        ]

    def arrived(copies):
        for copy in copies:
            copy.wait_recv()

    def left(copies):
        for copy in copies:
            copy.wait_send()

    def stream(h):
        columns = pl.ds(h * W, W)
        e_copies = []
        everything = []

        def send_shared(t):
            def gather(rows, base):
                e_send[h, rows] = halves(dot(from_slots[rows], two[h]))

            each_tile(2, NS, gather)
            e_copies.append(exchange(e_send.at[h], e_recv.at[h, t]))

        def receive_shared(t):
            arrived(e_copies[t])

            def cut(rows, base):
                e_two[rows] = split(e_recv[h, t, rows])

            each_tile(2, NS, cut)

        def scattered(rows):
            return halves(dot(to_slots[rows], e_two[...]))

        def modal_and_gather(t):
            modal = halves(dot(phit_hi[...], two[h]) + dot(phit_lo[...], two[h]))
            ag[h, t, xx] = modal
            return [send(ag.at[h, t, xx], ag.at[h, t, xx], x_peer(d)) for d in THREE]

        def reduce_x(t):
            return [send(ar_send.at[h, t, 0], ar_recv.at[h, t, i], x_peer(d)) for i, d in enumerate(THREE)]

        def reduce_z(t, copies):
            arrived(copies)
            ar_send[h, t, 1] = ar_send[h, t, 0] + ar_recv[h, t, 0] + ar_recv[h, t, 1] + ar_recv[h, t, 2]
            return [send(ar_send.at[h, t, 1], ar_recv.at[h, t, 3 + i], zy_peer(d, 0)) for i, d in enumerate(THREE)]

        def reduce_y(t, copies):
            arrived(copies)
            ar_send[h, t, 2] = ar_send[h, t, 1] + ar_recv[h, t, 3] + ar_recv[h, t, 4] + ar_recv[h, t, 5]
            return [send(ar_send.at[h, t, 2], ar_recv.at[h, t, 6 + i], yc_peer(*d)) for i, d in enumerate(YC)]

        def reduced(t, copies):
            arrived(copies)
            total = ar_send[h, t, 2]
            for i in range(7):
                total = total + ar_recv[h, t, 6 + i]
            numerator = jnp.sum(total[:8], axis=0, keepdims=True)
            denominator = jnp.sum(total[8:], axis=0, keepdims=True)
            return numerator / (denominator + 1e-06)

        send_shared(0)
        yield
        receive_shared(0)

        def first_residual(rows, base):
            value = w_buf[h, rows] + scattered(rows)
            r_out[rows, columns] = value
            two[h, rows] = split(value)

        each_tile(ROW_TILES, TILE, first_residual)
        ag_copies = modal_and_gather(0)
        yield

        rs_copies = []
        ar_x = ar_z = ar_y = None
        for t in range(ITERS):
            arrived(ag_copies)
            everything += ag_copies
            for i in range(4):
                ag_two[h, pl.ds(i * NM, NM)] = split(ag[h, t, i])
            left(rs_copies)
            rs_copies = []
            for pair in range(4):
                rows = pl.ds(pair * 256, 256)
                rs_send[h, rows] = halves(dot(c_hi[rows], ag_two[h]) + dot(c_lo[rows], ag_two[h]))
                for k in (2 * pair, 2 * pair + 1):
                    if k < 7:
                        rs_copies.append(
                            send(rs_send.at[h, pl.ds(k * NM, NM)], rs_recv.at[h, t, back(*ZY[k])], zy_peer(*ZY[k]))
                        )
            if t > 0:
                ar_z = reduce_z(t - 1, ar_x)
                everything += ar_x
            yield
            arrived(rs_copies)
            total = rs_send[h, pl.ds(7 * NM, NM)]
            for k in range(7):
                total = total + rs_recv[h, t, k]
            corr_w[h, t, 0] = total
            corr_copies = [
                send(corr_w.at[h, t, 0], corr_w.at[h, t, 1], ring(1)),
                send(corr_w.at[h, t, 0], corr_w.at[h, t, 2], ring(-1)),
            ]
            if t > 0:
                ar_y = reduce_y(t - 1, ar_z)
                everything += ar_z
            yield
            if t > 0:
                alpha = reduced(t - 1, ar_y)
                everything += ar_y
            arrived(corr_copies)
            everything += corr_copies
            for i in range(3):
                value = corr_w[h, t, i]
                if t > 0:
                    step = alpha * corr[h, i]
                    corr_sum[h, i] = step if t == 1 else corr_sum[h, i] + step
                    value = corr[h, i] - alpha * value
                corr[h, i] = value
                corr_two[h, pl.ds(i * NM, NM)] = split(value)

            def make_product(rows, base):
                value = smooth[rows, columns]
                if t > 0:
                    value = value - alpha * smooth_w[rows, columns]
                    smooth[rows, columns] = value
                    residual = r_out[rows, columns]
                    step = alpha * residual
                    x_out[rows, columns] = step if t == 1 else x_out[rows, columns] + step
                    r_out[rows, columns] = residual - alpha * w_buf[h, rows]
                value = value + halves(dot(b_hi[rows], corr_two[h]) + dot(b_lo[rows], corr_two[h]))
                value = jnp.where(live_mask(base, (TILE, W)), value, 0.0)
                w_buf[h, rows] = value
                two[h, rows] = split(value)

            each_tile(ROW_TILES, TILE, make_product)
            left(e_copies[t])
            send_shared(t + 1)
            yield
            receive_shared(t + 1)

            def make_image(i, sums):
                base = i * TILE
                rows = pl.ds(pl.multiple_of(base, TILE), TILE)
                value = w_buf[h, rows] + scattered(rows)
                w_buf[h, rows] = value
                if t < ITERS - 1:
                    two[h, rows] = split(value)
                    both = split(delta[rows] * value)
                    scaled_hi[rows, columns] = both[:, :W]
                    scaled_lo[rows, columns] = both[:, W:]
                weighted = share[rows] * value
                fold = lambda v: jnp.sum(v.reshape(TILE // 8, 8, W), axis=0)
                return (
                    sums[0] + fold(weighted * r_out[rows, columns]),
                    sums[1] + fold(weighted * value),
                )

            nothing = jnp.zeros((8, W), F32)
            numerator, denominator = lax.fori_loop(0, ROW_TILES, make_image, (nothing, nothing))
            ar_send[h, t, 0, pl.ds(0, 8)] = numerator
            ar_send[h, t, 0, pl.ds(8, 8)] = denominator
            ar_x = reduce_x(t)
            if t < ITERS - 1:
                ag_copies = modal_and_gather(t + 1)
            yield
        ar_z = reduce_z(ITERS - 1, ar_x)
        yield
        ar_y = reduce_y(ITERS - 1, ar_z)
        yield
        alpha = reduced(ITERS - 1, ar_y)

        def finish(rows, base):
            r_out[rows, columns] = r_out[rows, columns] - alpha * w_buf[h, rows]
            x_out[rows, columns] = x_out[rows, columns] + alpha * smooth_w[rows, columns]

        each_tile(ROW_TILES, TILE, finish)
        left(everything + ar_x + ar_z + ar_y + rs_copies + e_copies[ITERS])
        yield

    c_copies = [
        send(
            coarse.at[:, pl.ds(pl.multiple_of(zy_line(dz, dy) * 512, 512), 512)],
            c_in.at[back(dz, dy)],
            zy_peer(dz, dy),
        )
        for dz, dy in ZY[:-1]
    ]

    streams = [stream(h) for h in range(STREAMS)]

    def advance():
        for one in streams:
            next(one)

    advance()
    def build_rows(rows, base):
        local = lax.broadcasted_iota(jnp.int32, (TILE, NS), 0) + base
        counted = jnp.zeros((TILE, 1), F32)
        for side in range(2):
            hot = jnp.where(local == sides[side][...], 1.0, 0.0)
            to_slots[rows, pl.ds(side * NS, NS)] = hot.astype(BF16)
            counted = counted + jnp.sum(hot, axis=1, keepdims=True)
        alive = jnp.where(live_mask(base, (TILE, 1)), 1.0, 0.0)
        share[rows] = jnp.broadcast_to(alive / (1.0 + counted), (TILE, W))

    each_tile(ROW_TILES, TILE, build_rows)

    def cut_chunk(i, carry):
        chunk_copy(i).wait()
        slot = lax.rem(i, BUFFERS)
        base = pl.multiple_of(i * CHUNK, CHUNK)
        rows = pl.ds(base, CHUNK)
        for part in range(7):
            columns = pl.ds(part * 256, 256)
            value = chunk[slot, :, columns]
            high = value.astype(BF16)
            s_hi[rows, columns] = high
            s_lo[rows, columns] = (value - high.astype(F32)).astype(BF16)
        block = chunk[slot, :, pl.ds(base, CHUNK)]
        same = lax.broadcasted_iota(jnp.int32, (CHUNK, CHUNK), 0) == lax.broadcasted_iota(
            jnp.int32, (CHUNK, CHUNK), 1
        )
        diagonal = jnp.sum(jnp.where(same, block, 0.0), axis=1, keepdims=True)
        delta[rows] = share[rows] / diagonal
        return carry

    def cut_and_next(i, carry):
        cut_chunk(i, carry)
        chunk_copy(i + BUFFERS).start()
        return carry

    lax.fori_loop(0, CHUNKS - BUFFERS, cut_and_next, 0)
    lax.fori_loop(CHUNKS - BUFFERS, CHUNKS, cut_chunk, 0)

    loads[STREAMS].wait()
    mode_mask = lax.broadcasted_iota(jnp.int32, (256, NM), 1) < modes_live

    def weigh_modes(rows, base):
        value = jnp.where(mode_mask, share[rows] * phi[rows], 0.0)
        both = split(value)
        phi3_hi[rows, pl.ds(0, NM)] = both[:, :NM]
        phi3_lo[rows, pl.ds(0, NM)] = both[:, NM:]
        turned = value.T
        high = turned.astype(BF16)
        phit_hi[:, rows] = high
        phit_lo[:, rows] = (turned - high.astype(F32)).astype(BF16)
        scale = split(delta[rows])
        scaled_hi[rows] = jnp.concatenate([both[:, :NM], scale[:, :NM]], axis=1)
        scaled_lo[rows] = jnp.concatenate([both[:, NM:], scale[:, NM:]], axis=1)

    each_tile(7, 256, weigh_modes)

    def gather_pair(rows, base):
        hot = from_slots[rows]
        pair_send[rows] = dot(hot, scaled_hi[...]) + dot(hot, scaled_lo[...])

    each_tile(2, NS, gather_pair)
    pair_copies = exchange(pair_send, pair_recv)

    advance()

    arrived(pair_copies)

    def cut_pair(rows, base):
        value = pair_recv[rows]
        high = value.astype(BF16)
        scaled_hi[rows] = high
        scaled_lo[rows] = (value - high.astype(F32)).astype(BF16)

    each_tile(2, NS, cut_pair)

    def place_pair(rows, base):
        for side in range(2):
            slots = pl.ds(side * NS, NS)
            hot = to_slots[rows, slots]
            high = dot(hot, scaled_hi[slots])
            low = dot(hot, scaled_lo[slots])
            columns = pl.ds((1 + side) * NM, NM)
            phi3_hi[rows, columns] = high[:, :NM].astype(BF16)
            phi3_lo[rows, columns] = low[:, :NM].astype(BF16)
            delta[rows] = delta[rows] + (high[:, NM:] + low[:, NM:])

    each_tile(ROW_TILES, TILE, place_pair)

    def scale_residual(rows, base):
        for h in range(STREAMS):
            columns = pl.ds(h * W, W)
            both = split(delta[rows] * r_out[rows, columns])
            scaled_hi[rows, columns] = both[:, :W]
            scaled_lo[rows, columns] = both[:, W:]

    each_tile(ROW_TILES, TILE, scale_residual)

    def smoother(target, first, last):
        def tile(i, carry):
            rows = pl.ds(pl.multiple_of(i * TILE, TILE), TILE)
            target[rows] = (
                dot(s_hi[rows], scaled_hi[...]) + dot(s_hi[rows], scaled_lo[...]) + dot(s_lo[rows], scaled_hi[...])
            )
            return carry

        lax.fori_loop(first, last, tile, 0)

    def schur_modes(first, last):
        def tile(i, carry):
            rows = pl.ds(pl.multiple_of(i * TILE, TILE), TILE)
            value = halves(dot(s_hi[rows], phi3[...])) + dot(s_lo[rows], phi3_hi[...])
            high = value.astype(BF16)
            b_hi[rows] = high
            b_lo[rows] = (value - high.astype(F32)).astype(BF16)
            return carry

        lax.fori_loop(first, last, tile, 0)

    smoother(smooth, 0, 2)
    loads[STREAMS + 1].wait()
    arrived(c_copies)
    for k in range(8):
        both = split(c_in[k])
        c_hi[pl.ds(k * NM, NM)] = both[:, :512]
        c_lo[pl.ds(k * NM, NM)] = both[:, 512:]
    advance()
    smoother(smooth, 2, 4)
    schur_modes(0, 2)
    advance()
    schur_modes(2, 4)
    advance()
    for t in range(1, ITERS):
        advance()
        smoother(smooth_w, 0, 1)
        advance()
        smoother(smooth_w, 1, 3)
        advance()
        smoother(smooth_w, 3, 4)
        advance()

    for h in range(STREAMS):
        columns = pl.ds(h * W, W)
        for i in range(3):
            sum_two[pl.ds(i * NM, NM)] = split(corr_sum[h, i])

        def prolong(rows, base):
            high, low = phi3_hi[rows], phi3_lo[rows]
            x_out[rows, columns] = delta[rows] * x_out[rows, columns] + halves(
                dot(high, sum_two[...]) + dot(low, sum_two[...])
            )
            smooth_w[rows, columns] = delta[rows] * r_out[rows, columns] + halves(
                dot(high, corr_two[h]) + dot(low, corr_two[h])
            )

        each_tile(ROW_TILES, TILE, prolong)
    for _ in range(4):
        advance()
    left(c_copies)
    left(pair_copies)


def local(load, schur, modes, coarse_inverse, interface_rows, mode_count, left_rows, right_rows):
    vmem = pl.BlockSpec(memory_space=pltpu.VMEM)
    smem = pl.BlockSpec(memory_space=pltpu.SMEM)
    anywhere = pl.BlockSpec(memory_space=pl.ANY)
    copies = 7 + 2 + STREAMS * (2 * (ITERS + 1) + ITERS * (3 + 7 + 2 + 3 + 3 + 7))
    return pl.pallas_call(
        kernel,
        out_shape=(jax.ShapeDtypeStruct((NI, K), F32), jax.ShapeDtypeStruct((NI, K), F32)),
        in_specs=[anywhere, anywhere, anywhere, anywhere, smem, smem, vmem, vmem],
        out_specs=(vmem, vmem),
        scratch_shapes=[
            pltpu.VMEM((NI, NI), BF16),
            pltpu.VMEM((NI, NI), BF16),
            pltpu.VMEM((BUFFERS, CHUNK, NI), F32),
            pltpu.VMEM((NI, 2 * NS), BF16),
            pltpu.VMEM((2 * NS, NI), BF16),
            pltpu.VMEM((NI, NM), F32),
            pltpu.VMEM((NM, NI), BF16),
            pltpu.VMEM((NM, NI), BF16),
            pltpu.VMEM((NI, 6 * NM), BF16),
            pltpu.VMEM((NI, 3 * NM), BF16),
            pltpu.VMEM((NI, 3 * NM), BF16),
            pltpu.VMEM((8, NM, 512), F32),
            pltpu.VMEM((8 * NM, 512), BF16),
            pltpu.VMEM((8 * NM, 512), BF16),
            pltpu.VMEM((NI, W), F32),
            pltpu.VMEM((NI, W), F32),
            pltpu.VMEM((2 * NS, 2 * NM), F32),
            pltpu.VMEM((2 * NS, 2 * NM), F32),
            pltpu.VMEM((STREAMS, NI, W), F32),
            pltpu.VMEM((NI, K), BF16),
            pltpu.VMEM((NI, K), BF16),
            pltpu.VMEM((NI, K), F32),
            pltpu.VMEM((NI, K), F32),
            pltpu.VMEM((STREAMS, NI, 2 * W), BF16),
            pltpu.VMEM((2 * NS, 2 * W), BF16),
            pltpu.VMEM((STREAMS, 2 * NS, W), F32),
            pltpu.VMEM((STREAMS, ITERS + 1, 2 * NS, W), F32),
            pltpu.VMEM((STREAMS, ITERS, 4, NM, W), F32),
            pltpu.VMEM((STREAMS, 4 * NM, 2 * W), BF16),
            pltpu.VMEM((STREAMS, 8 * NM, W), F32),
            pltpu.VMEM((STREAMS, ITERS, 7, NM, W), F32),
            pltpu.VMEM((STREAMS, 3, NM, W), F32),
            pltpu.VMEM((STREAMS, ITERS, 3, NM, W), F32),
            pltpu.VMEM((STREAMS, 3, NM, W), F32),
            pltpu.VMEM((STREAMS, 3 * NM, 2 * W), BF16),
            pltpu.VMEM((3 * NM, 2 * W), BF16),
            pltpu.VMEM((STREAMS, ITERS, 3, 16, W), F32),
            pltpu.VMEM((STREAMS, ITERS, 13, 16, W), F32),
            pltpu.SemaphoreType.DMA((STREAMS + 2,)),
            pltpu.SemaphoreType.DMA((BUFFERS,)),
            pltpu.SemaphoreType.DMA((copies,)),
            pltpu.SemaphoreType.DMA((copies,)),
        ],
        compiler_params=pltpu.CompilerParams(
            collective_id=0, has_side_effects=True, vmem_limit_bytes=62 * 1024 * 1024
        ),
        cost_estimate=pl.CostEstimate(flops=20 * 10**9, bytes_accessed=21 * 10**6, transcendentals=0),
    )(load, schur, modes, coarse_inverse, interface_rows, mode_count, left_rows, right_rows)


def solution(mesh):
    return jax.shard_map(
        local,
        mesh=mesh,
        in_specs=(
            P(("cluster", "sub"), None),
            P(("cluster", "sub"), None),
            P(("cluster", "sub"), None),
            P(("cluster", "sub"), None),
            P(("cluster", "sub")),
            P(("cluster", "sub")),
            P(("cluster", "sub"), None),
            P(("cluster", "sub"), None),
        ),
        out_specs=(P(("cluster", "sub"), None), P(("cluster", "sub"), None)),
        check_vma=False,
    )
```
